32 devices in a mesh: fsdp: 4 (over y, x), rep: 8 (over z, core).
Axes of the slice: x: 2, y: 2, z: 4, core: 2. Of those that a mesh axis runs over, the one named last changes fastest.
Arguments:
- inputs: bfloat16 [1, 28672, 1280], P(None, ('fsdp', 'rep')), may hold values from -6 to 6
- cotangent: bfloat16 [1, 28672, 1280], P(None, ('fsdp', 'rep')), may hold values from -6 to 6
- lengths: int32 [1, 32], replicated, may hold values from 560 to 896
- threshold: int32 [1], replicated, may hold values from 8 to 48
- w_query: bfloat16 [1280, 1280], P('fsdp'), may hold values from -1 to 1
- w_key: bfloat16 [1280, 1280], P('fsdp'), may hold values from -0.15625 to 0.15625
- w_value: bfloat16 [1280, 1280], P('fsdp'), may hold values from -0.15625 to 0.15625
- w_out: bfloat16 [1280, 1280], P('fsdp'), may hold values from -1.25 to 1.25
- w_up: bfloat16 [1280, 5120], P('fsdp'), may hold values from -0.15625 to 0.15625
- w_down: bfloat16 [5120, 1280], P('fsdp'), may hold values from -0.078125 to 0.078125
- b_query: bfloat16 [1280], P('fsdp'), may hold values from -1.75 to 1.75
- b_value: bfloat16 [1280], P('fsdp'), may hold values from -3 to 3
- b_out: bfloat16 [1280], P('fsdp'), may hold values from -3 to 3
- b_up: bfloat16 [5120], P('fsdp'), may hold values from -3 to 3
- b_down: bfloat16 [1280], P('fsdp'), may hold values from -3 to 3
- gain_attn: bfloat16 [1280], P('fsdp'), may hold values from 0.25 to 1.75
- shift_attn: bfloat16 [1280], P('fsdp'), may hold values from -1.75 to 1.75
- gain_ffn: bfloat16 [1280], P('fsdp'), may hold values from 0.25 to 1.75
- shift_ffn: bfloat16 [1280], P('fsdp'), may hold values from -1.75 to 1.75
Outputs:
- layer_out: bfloat16 [1, 28672, 1280], P(None, ('fsdp', 'rep'))
- grad_inputs: float32 [1, 28672, 1280], P(None, ('fsdp', 'rep'))
- grad_w_query: float32 [1280, 1280], P('fsdp')
- grad_w_key: float32 [1280, 1280], P('fsdp')
- grad_w_value: float32 [1280, 1280], P('fsdp')
- grad_w_out: float32 [1280, 1280], P('fsdp')
- grad_w_up: float32 [1280, 5120], P('fsdp')
- grad_w_down: float32 [5120, 1280], P('fsdp')
- grad_b_query: float32 [1280], P('fsdp')
- grad_b_value: float32 [1280], P('fsdp')
- grad_b_out: float32 [1280], P('fsdp')
- grad_b_up: float32 [5120], P('fsdp')
- grad_b_down: float32 [1280], P('fsdp')
- grad_gain_attn: float32 [1280], P('fsdp')
- grad_shift_attn: float32 [1280], P('fsdp')
- grad_gain_ffn: float32 [1280], P('fsdp')
- grad_shift_ffn: float32 [1280], P('fsdp')
- head_peak: float32 [16], replicated
- clip_factor: float32 [16], replicated
- clipped_query: bfloat16 [1280, 1280], P('fsdp')
- clipped_key: bfloat16 [1280, 1280], P('fsdp')
The draws below stay inside these ranges and needn't reach their ends.
All inputs are finite; a program needn't handle non-finite values.
Results may differ from the reference program's by a relative error of at most 0.019.
Values may be sent and summed in bfloat16 or wider, within the bound.
No kernel may reach another device: no remote copies, remote signals or barrier semaphores. Data moves between devices by JAX's collectives and lax.ppermute only.
A program may use at most 320 MiB of HBM per device.

```python
import math
import jax
import jax.numpy as jnp
from jax import lax

D = 1280
H = 16
HD = 80
FF = 5120
LEN = 896
CLIPS_DEV = 1
DEVICES = 32


def draw_w_query(key, part):
    head_scale = jnp.exp(jax.random.uniform(jax.random.fold_in(key, 11), (H,), minval=0.0, maxval=math.log(2.2)))
    base_draw = jax.random.truncated_normal(jax.random.fold_in(key, 12), -6.0, 6.0, (D, D))
    column_scale = jnp.repeat(head_scale, HD, total_repeat_length=D)
    return (base_draw * column_scale[None, :] * D ** (-0.5)).astype(jnp.bfloat16)


def plant(drawn, stream_key, least, largest):
    spot = [jax.random.randint(jax.random.fold_in(stream_key, axis), (), 0, length) for axis, length in enumerate(drawn.shape)]
    widest = drawn.shape.index(max(drawn.shape))
    neighbour = spot[:widest] + [(spot[widest] + 1) % drawn.shape[widest]] + spot[widest + 1:]
    return drawn.at[tuple(spot)].set(least).at[tuple(neighbour)].set(largest)


def levels(rng, dims, shards, low, top_value):
    def one(position, shards_of):
        heights = jax.random.uniform(jax.random.fold_in(jax.random.fold_in(rng, 6), position), (shards_of,), jnp.float32, low / len(shards), top_value / len(shards))
        return jnp.repeat(jnp.exp(heights), dims[position] // shards_of).reshape((-1,) + (1,) * (len(dims) - position - 1))

    level = one(*shards[0])
    for cut in shards[1:]:
        level = level * one(*cut)
    return level


def noise(key, shape, scale, reach, cuts=(), held_as=jnp.bfloat16):
    drawn = jax.random.normal(key, shape, jnp.float32) * scale
    if len(cuts) > 0:
        drawn = levels(key, shape, cuts, -0.22, 0.18) * drawn
    return jnp.clip(drawn, min=-reach, max=reach).astype(held_as)


def setup_inputs(seed: int = 0) -> dict:
    arg_keys = jax.random.split(jax.random.key(seed), 20)
    return {
        "inputs": noise(arg_keys[0], (CLIPS_DEV, DEVICES * LEN, D), 1.0, 6.0, ((1, 32),)),
        "cotangent": noise(arg_keys[1], (CLIPS_DEV, DEVICES * LEN, D), 1.0, 6.0, ((1, 32),)),
        "lengths": plant(jax.random.randint(arg_keys[2], (CLIPS_DEV, DEVICES), 5 * LEN // 8, LEN + 1), jax.random.fold_in(arg_keys[2], 1), 5 * LEN // 8, LEN).astype(jnp.int32),
        "threshold": jax.random.randint(arg_keys[3], (1,), 8, 49).astype(jnp.int32),
        "w_query": draw_w_query(jax.random.fold_in(arg_keys[19], 71), 0),
        "w_key": noise(arg_keys[5], (D, D), D ** -0.5, 0.15625, ((0, 4),)),
        "w_value": noise(arg_keys[6], (D, D), D ** -0.5, 0.15625, ((0, 4),)),
        "w_out": noise(arg_keys[7], (D, D), (D // 64) ** -0.5, 1.25, ((0, 4),)),
        "w_up": noise(arg_keys[8], (D, FF), D ** -0.5, 0.15625, ((0, 4),)),
        "w_down": noise(arg_keys[9], (FF, D), FF ** -0.5, 0.078125, ((0, 4),)),
        "b_query": noise(arg_keys[10], (D,), 0.3, 1.75, ((0, 4),)),
        "b_value": noise(arg_keys[11], (D,), 0.5, 3.0, ((0, 4),)),
        "b_out": noise(arg_keys[12], (D,), 0.5, 3.0, ((0, 4),)),
        "b_up": noise(arg_keys[13], (FF,), 0.5, 3.0, ((0, 4),)),
        "b_down": noise(arg_keys[14], (D,), 0.5, 3.0, ((0, 4),)),
        "gain_attn": jnp.clip(1.0 + 0.15 * jax.random.normal(arg_keys[15], (D,), jnp.float32), 0.25, 1.75).astype(jnp.bfloat16),
        "shift_attn": noise(arg_keys[16], (D,), 0.3, 1.75, ((0, 4),)),
        "gain_ffn": jnp.clip(1.0 + 0.15 * jax.random.normal(arg_keys[17], (D,), jnp.float32), 0.25, 1.75).astype(jnp.bfloat16),
        "shift_ffn": noise(arg_keys[18], (D,), 0.3, 1.75, ((0, 4),)),
    }


@jax.custom_vjp
def low(v):
    return lax.optimization_barrier(v.astype(jnp.bfloat16)).astype(jnp.float32)

@jax.custom_vjp
def low_back(v):
    return v

def low_keep(v):
    return (low(v), None)

def low_pass(kept, grad):
    return (grad,)

def back_keep(v):
    return (v, None)

def back_low(kept, grad):
    return (low(grad),)
low.defvjp(low_keep, low_pass)
low_back.defvjp(back_keep, back_low)
epsilon = 1e-05
masked_value = -1e+30
threshold_unit = 16.0

def layer_norm(values, gain_vec, shift_vec):
    centre = values - lax.optimization_barrier(jnp.mean(values, axis=-1, keepdims=True))
    spread = lax.optimization_barrier(jnp.mean(centre * centre, axis=-1, keepdims=True))
    return centre * lax.rsqrt(spread + epsilon) * gain_vec + shift_vec

def rounded(values):
    return low_back(low(values))

def product(left, right):
    return jnp.dot(left, right, precision=lax.Precision.HIGHEST, preferred_element_type=jnp.float32)

def clip_layer(weights, frames, valid_len):
    w_query, w_key, w_value, w_out, w_up, w_down, b_query, b_value, b_out, b_up, b_down, gain_attn, shift_attn, gain_ffn, shift_ffn = weights
    normed = low(layer_norm(frames, gain_attn, shift_attn))
    queries = rounded(product(normed, w_query) + b_query).reshape(LEN, H, HD)
    key_rows = rounded(product(normed, w_key)).reshape(LEN, H, HD)
    value_rows = rounded(product(normed, w_value) + b_value).reshape(LEN, H, HD)
    raw_scores = low_back(jnp.einsum('qhd,khd->hqk', queries, key_rows, precision=lax.Precision.HIGHEST))
    scores = raw_scores * HD ** (-0.5)
    visible = jnp.arange(LEN, dtype=jnp.int32) < valid_len
    scores = jnp.where(visible[None, None, :], scores, masked_value)
    head_peak = lax.optimization_barrier(jnp.max(scores, axis=(1, 2)))
    probabilities = low(jax.nn.softmax(scores, axis=-1))
    mixed_rows = rounded(jnp.einsum('hqk,khd->qhd', probabilities, value_rows, precision=lax.Precision.HIGHEST).reshape(LEN, D))
    middle = frames + low_back(product(mixed_rows, w_out) + b_out)
    normed_ffn = low(layer_norm(middle, gain_ffn, shift_ffn))
    hidden = low(jax.nn.gelu(low_back(product(normed_ffn, w_up) + b_up), approximate=False))
    return (middle + low_back(product(hidden, w_down) + b_down), head_peak)

def forward(weights, frames, lengths):
    clip_rows = frames.reshape(CLIPS_DEV * DEVICES, LEN, D)
    valid_all = lengths.reshape(CLIPS_DEV * DEVICES)

    def one_clip(packed):
        return clip_layer(weights, packed[0], packed[1])
    results, peaks = lax.map(jax.checkpoint(one_clip), (clip_rows, valid_all))
    return (results.reshape(CLIPS_DEV, DEVICES * LEN, D), lax.optimization_barrier(jnp.max(peaks, axis=0)))

def reference(inputs, cotangent, lengths, threshold, w_query, w_key, w_value, w_out, w_up, w_down, b_query, b_value, b_out, b_up, b_down, gain_attn, shift_attn, gain_ffn, shift_ffn):
    weights = tuple((initial.astype(jnp.float32) for initial in (w_query, w_key, w_value, w_out, w_up, w_down, b_query, b_value, b_out, b_up, b_down, gain_attn, shift_attn, gain_ffn, shift_ffn)))
    frames = inputs.astype(jnp.float32)

    def forward_run(weights_in, frames_in):
        return forward(weights_in, frames_in, lengths)
    layer_out, pull_back, head_peak = jax.vjp(forward_run, weights, frames, has_aux=True)
    weight_grads, input_grad = pull_back(cotangent.astype(jnp.float32))
    clip_limit = threshold[0].astype(jnp.float32) / threshold_unit
    factor = jnp.sqrt(clip_limit / jnp.maximum(head_peak, clip_limit))
    columns = jnp.repeat(factor, HD)
    clipped_query = (weights[0] * columns[None, :]).astype(jnp.bfloat16)
    clipped_key = (weights[1] * columns[None, :]).astype(jnp.bfloat16)
    return (layer_out.astype(jnp.bfloat16), input_grad, weight_grads[0], weight_grads[1], weight_grads[2], weight_grads[3], weight_grads[4], weight_grads[5], weight_grads[6], weight_grads[7], weight_grads[8], weight_grads[9], weight_grads[10], weight_grads[11], weight_grads[12], weight_grads[13], weight_grads[14], head_peak, factor, clipped_query, clipped_key)
```

```python
import functools

import jax
import jax.numpy as jnp
from jax import lax
from jax.experimental import pallas as pl
from jax.experimental.pallas import tpu as pltpu
from jax.sharding import PartitionSpec as P

H = 16
HD = 80
EPS = 1e-05
UNIT = 16.0
SCALE = HD ** (-0.5)
LOG2E = 1.4426950408889634
F32 = jnp.float32
BF = jnp.bfloat16
AXES = ("fsdp", "rep")
MIB = 1024 * 1024
VMEM = dict(
    unpack_vectors=8,
    pack_vectors=8,
    merge=4,
    pick=8,
    land=2,
    combine=16,
    assemble=20,
    norm_attn=8,
    project=20,
    attend=28,
    attend_back=36,
    out_project=44,
    up_project=32,
    down_back=44,
    down_project=44,
    up_back=52,
    out_back=24,
    input_back=44,
    wgrad_down=32,
    wgrad_up=40,
    wgrad_out=24,
    wgrad_qkv=44,
)


def dg(a, b, ca, cb):
    return lax.dot_general(a, b, (((ca,), (cb,)), ((), ())), preferred_element_type=F32)


class Clock:
    def __init__(self, on):
        self.on, self.deps, self.last, self.soon = on, [], [], []

    def wait(self, *values):
        self.deps += values

    def after_next(self, v):
        self.soon.append(v)
        return v

    def take(self):
        deps = self.deps + self.last if self.on else []
        self.deps, self.soon = self.soon, []
        return deps


CLOCK = [Clock(False)]


def pcall(kernel, *, out_shape, grid_spec=None, grid=None, in_specs=None, out_specs=None,
          deps=None, aliases=None, cost_estimate=None, name=None):
    spec = grid_spec or dict(grid=grid, in_specs=in_specs, out_specs=out_specs)
    npre = spec.get("num_scalar_prefetch", 0)
    nin = npre + len(spec["in_specs"])
    chained = deps is None
    deps = CLOCK[0].take() if chained else list(deps)
    spec = dict(spec, in_specs=list(spec["in_specs"]) + [ANY] * len(deps))
    spec["num_scalar_prefetch"] = npre

    def body(*refs):
        kernel(*refs[:nin], *refs[nin + len(deps) :])

    f = pl.pallas_call(
        body,
        grid_spec=pltpu.PrefetchScalarGridSpec(**spec),
        out_shape=out_shape,
        input_output_aliases=aliases or {},
        compiler_params=pltpu.CompilerParams(
            dimension_semantics=("arbitrary",) * len(spec["grid"]),
            vmem_limit_bytes=VMEM[name] * MIB,
        ),
        cost_estimate=cost_estimate,
        name=name,
    )

    def run(*args):
        out = f(*args, *deps)
        if chained:
            CLOCK[0].last = [jax.tree.leaves(out)[0]]
        return out

    return run


PACE = 1.0
COST = dict(wgrad_down=8, wgrad_up=9, wgrad_out=5, wgrad_qkv=9)


def cost(us):
    return pl.CostEstimate(
        flops=int(us * PACE * 1.15e9), bytes_accessed=1024, transcendentals=0
    )


def full(shape):
    return pl.BlockSpec(shape, lambda *_: (0,) * len(shape))


ANY = pl.BlockSpec(memory_space=pltpu.HBM)


class Weight:
    def __init__(self, chunks, width, rows, offs):
        self.chunks, self.width, self.rows, self.offs = chunks, width, rows, offs
        self.cols = width * len(chunks)
        self.total = None
        self.arrays = [a for arrays, _ in chunks for a in arrays]

    def copies(self, refs, offs, buf, sem, lo, hi, at=0):
        out = []
        k = len(self.rows)
        for c, (_, base) in enumerate(self.chunks):
            a, b = max(lo, c * self.width), min(hi, (c + 1) * self.width)
            if a >= b:
                continue
            for i in range(k):
                start = a - c * self.width + base[i]
                out.append(
                    pltpu.make_async_copy(
                        refs[c * k + i].at[:, pl.ds(start, b - a)],
                        buf.at[
                            pl.ds(pl.multiple_of(offs[i], 16), self.rows[i]),
                            pl.ds(at + a - lo, b - a),
                        ],
                        sem.at[len(out)],
                    )
                )
        return out


def start_all(copies):
    for c in copies:
        c.start()


def wait(copies):
    for c in copies:
        c.wait()


def stream(w, refs, offs, buf, sem, tile, j):
    nt = w.cols // tile

    def copies(i):
        return w.copies(refs, offs, buf.at[i % 2], sem.at[i % 2], i * tile, (i + 1) * tile)

    for i in range(nt):

        @pl.when(j == i)
        def _(i=i):
            if i == 0:
                start_all(copies(0))
            if i + 1 < nt:
                start_all(copies(i + 1))
            wait(copies(i))

    return lax.rem(j, 2)


def chunks_of(rows, step=128):
    return [(r, min(step, rows - r)) for r in range(0, rows, step)]


def groups_of(rows):
    first = 256
    second = (rows - first) // 256 * 128
    return [(0, first), (first, second), (first + second, rows - first - second)]


def absolute(f, items):
    a, b, c, d = items
    odd = f % 2 == 1
    a, b = jnp.where(odd, b, a), jnp.where(odd, a, b)
    c, d = jnp.where(odd, d, c), jnp.where(odd, c, d)
    high = f // 2 == 1
    return [
        jnp.where(high, c, a),
        jnp.where(high, d, b),
        jnp.where(high, a, c),
        jnp.where(high, b, d),
    ]


def unpack_vectors(shards, k, ku, f=None):
    n = len(shards)
    npre = 0 if f is None else 1

    def kernel(*rest):
        rows_ref, cols_ref, up_ref = rest[npre + n :]
        parts = [r[...].astype(F32) for r in rest[npre : npre + n]]
        if npre:
            parts = absolute(rest[0][0], parts)
        rows = [
            jnp.concatenate([p[:, i * k : (i + 1) * k] for p in parts], axis=1) for i in range(8)
        ]
        rows = jnp.concatenate(rows, axis=0)
        rows_ref[...] = rows
        cols_ref[...] = jnp.transpose(rows)
        up_ref[...] = jnp.concatenate([p[:, 8 * k : 8 * k + ku] for p in parts], axis=1)

    width = shards[0].shape[1]
    return pcall(
        kernel,
        grid_spec=dict(
            num_scalar_prefetch=npre,
            grid=(1,),
            in_specs=[full((1, width))] * n,
            out_specs=[full((8, n * k)), full((n * k, 8)), full((1, n * ku))],
        ),
        out_shape=[
            jax.ShapeDtypeStruct((8, n * k), F32),
            jax.ShapeDtypeStruct((n * k, 8), F32),
            jax.ShapeDtypeStruct((1, n * ku), F32),
        ],
            cost_estimate=cost(2),
        name="unpack_vectors",
    )(*([] if f is None else [f]), *shards)


def pack_vectors(f, n, first, sums_qkv, sums_ffn, sums_attn, grad_bd, grad_bu, stats):
    d = sums_ffn.shape[1]
    k, ku = d // n, grad_bu.shape[1] // n
    half = d // 2
    width = 8 * k + ku + 128

    def kernel(f_ref, first_ref, a_ref, b_ref, ffn_ref, attn_ref, bd_ref, bu_ref, st_ref, *outs):
        low = first_ref[0] == 0

        def row(i):
            a = jnp.transpose(a_ref[i])[0:1, :]
            b = jnp.transpose(b_ref[i])[0:1, :]
            return jnp.concatenate([jnp.where(low, a, b), jnp.where(low, b, a)], axis=1)

        rows = [
            row(0),
            row(1),
            ffn_ref[2:3, :],
            bd_ref[...],
            attn_ref[0:1, :],
            attn_ref[1:2, :],
            ffn_ref[0:1, :],
            ffn_ref[1:2, :],
        ]
        tops = jnp.max(st_ref[:, 1, :], axis=1, keepdims=True)
        tops = jnp.concatenate([jnp.broadcast_to(tops, (H, 128)), jnp.zeros((128 - H, 128), F32)])
        tops = jnp.transpose(tops)[0:1, :]
        owners = [
            jnp.concatenate(
                [r[:, i * k : (i + 1) * k] for r in rows]
                + [bu_ref[:, i * ku : (i + 1) * ku], tops],
                axis=1,
            )
            for i in range(n)
        ]
        if n == 4:
            owners = absolute(f_ref[0], owners)
        for o_ref, v in zip(outs, owners):
            o_ref[...] = v

    args = [*sums_qkv, sums_ffn, sums_attn, grad_bd, grad_bu, stats]
    return pcall(
        kernel,
        grid_spec=dict(
            num_scalar_prefetch=2,
            grid=(1,),
            in_specs=[full(a.shape) for a in args],
            out_specs=[full((1, width))] * n,
        ),
        out_shape=[jax.ShapeDtypeStruct((1, width), F32)] * n,
            cost_estimate=cost(2.7),
        name="pack_vectors",
    )(f, first, *args)


def norm_kernel(x_ref, v_ref, o_ref):
    v = x_ref[...].astype(F32)
    c = v - jnp.mean(v, axis=1, keepdims=True)
    r = lax.rsqrt(jnp.mean(c * c, axis=1, keepdims=True) + EPS)
    y = c * r * v_ref[4:5, :] + v_ref[5:6, :]
    o_ref[...] = jnp.transpose(y).astype(BF)


def norm_transposed(x, vrows):
    t, d = x.shape
    return pcall(
        norm_kernel,
        grid=(t // 128,),
        in_specs=[pl.BlockSpec((128, d), lambda i: (i, 0)), full((8, d))],
        out_specs=pl.BlockSpec((d, 128), lambda i: (0, i)),
        out_shape=jax.ShapeDtypeStruct((d, t), BF),
            cost_estimate=cost(6.7),
        name="norm_attn",
    )(x, vrows)


def project(w, xt, cols, col, tile=640):
    d, t = xt.shape
    n = w.cols
    k = len(w.arrays)

    def kernel(offs, x_ref, b_ref, *rest):
        refs = rest[:k]
        o_ref, buf, sem = rest[k:]
        slot = stream(w, refs, offs, buf, sem, tile, pl.program_id(0))
        out = dg(buf[slot], x_ref[...], 0, 0)
        if col is not None:
            out = out + b_ref[:, col : col + 1]
        o_ref[...] = out.astype(BF)

    return pcall(
        kernel,
        grid_spec=dict(
            num_scalar_prefetch=1,
            grid=(n // tile,),
            in_specs=[full((d, t)), pl.BlockSpec((tile, 8), lambda j, o: (j, 0))] + [ANY] * k,
            out_specs=pl.BlockSpec((tile, t), lambda j, o: (j, 0)),
            scratch_shapes=[pltpu.VMEM((2, d, tile), BF), pltpu.SemaphoreType.DMA((2, k))],
        ),
        out_shape=jax.ShapeDtypeStruct((n, t), BF),
            cost_estimate=cost(8.8),
        name="project",
    )(w.offs, xt, cols, *w.arrays)


HPG = 2


def attend_kernel(len_ref, q_ref, k_ref, v_ref, mixed_ref, stat_ref):
    t = q_ref.shape[1]
    row = lax.broadcasted_iota(jnp.int32, (16, t), 0)
    pos = lax.broadcasted_iota(jnp.int32, (16, t), 1)
    hidden = jnp.where((row == 0) & (pos >= len_ref[0]), -1e30, 0.0).astype(BF)
    ones = jnp.ones((16, t), BF)
    for g in range(HPG):
        rows = slice(g * HD, (g + 1) * HD)
        keys = jnp.concatenate([k_ref[rows, :], hidden], axis=0)
        queries = jnp.concatenate([q_ref[rows, :], ones], axis=0)
        values = jnp.concatenate([v_ref[rows, :], ones], axis=0)
        raw = dg(keys, queries, 0, 0)
        top = jnp.max(raw, axis=0, keepdims=True)
        expo = jnp.exp2((raw - top) * (SCALE * LOG2E)).astype(BF)
        out = dg(values, expo, 1, 0)
        total = out[HD : HD + 1, :]
        mixed_ref[rows, :] = (out[:HD, :] / total).astype(BF)
        stat_ref[g, 0:1, :] = top + jnp.log2(total) * (1.0 / (SCALE * LOG2E))
        stat_ref[g, 1:2, :] = top * SCALE
        stat_ref[g, 2:8, :] = jnp.zeros((6, t), F32)


def attend(valid, qt, kt, vt):
    d, t = qt.shape
    blk = pl.BlockSpec((HPG * HD, t), lambda i, o: (i, 0))
    return pcall(
        attend_kernel,
        grid_spec=dict(
            num_scalar_prefetch=1,
            grid=(H // HPG,),
            in_specs=[blk] * 3,
            out_specs=[blk, pl.BlockSpec((HPG, 8, t), lambda i, o: (i, 0, 0))],
        ),
        out_shape=[
            jax.ShapeDtypeStruct((d, t), BF),
            jax.ShapeDtypeStruct((H, 8, t), F32),
        ],
            cost_estimate=cost(21),
        name="attend",
    )(valid, qt, kt, vt)


def three_rows(v):
    hi = v.astype(BF).astype(F32)
    mid = (v - hi).astype(BF).astype(F32)
    low = (v - hi - mid).astype(BF).astype(F32)
    return [hi, mid, low]


def attend_back_kernel(
    len_ref, half_ref, q_ref, k_ref, v_ref, m_ref, dm_ref, stat_ref, o_ref, sum_ref
):
    t = q_ref.shape[1]
    row = lax.broadcasted_iota(jnp.int32, (16, t), 0)
    pos = lax.broadcasted_iota(jnp.int32, (16, t), 1)
    key_rows = jnp.where(
        row < 3, 1.0, jnp.where((row == 3) & (pos >= len_ref[0]), -1e30, 0.0)
    ).astype(BF)
    value_rows = jnp.where(row < 3, 1.0, 0.0).astype(BF)
    one = jnp.ones((1, t), F32)
    zeros = jnp.zeros((12, t), F32)
    for g in range(HPG):
        rows = slice(g * HD, (g + 1) * HD)
        qt, kt, vt, dm = q_ref[rows, :], k_ref[rows, :], v_ref[rows, :], dm_ref[rows, :]
        inner = jnp.sum(dm.astype(F32) * m_ref[rows, :].astype(F32), axis=0, keepdims=True)
        q_rows = jnp.concatenate(three_rows(-stat_ref[g, 0:1, :]) + [one, zeros], axis=0)
        d_rows = jnp.concatenate(three_rows(-inner) + [one, zeros], axis=0)
        shifted = dg(
            jnp.concatenate([qt, q_rows.astype(BF)], axis=0),
            jnp.concatenate([kt, key_rows], axis=0),
            0,
            0,
        )
        probs = jnp.exp2(shifted * (SCALE * LOG2E))
        grad_probs = dg(
            jnp.concatenate([dm, d_rows.astype(BF)], axis=0),
            jnp.concatenate([vt, value_rows], axis=0),
            0,
            0,
        )
        grad_scores = (probs * grad_probs).astype(BF)
        grad_v = dg(dm, probs.astype(BF), 1, 0).astype(BF)
        grad_k = (dg(qt, grad_scores, 1, 0) * SCALE).astype(BF)
        grad_q = (dg(kt, grad_scores, 1, 1) * SCALE).astype(BF)
        o_ref[0, rows, :] = grad_q
        o_ref[1, rows, :] = grad_k
        o_ref[2, rows, :] = grad_v
        for i, v in enumerate((grad_q, grad_v)):
            total = jnp.sum(v.astype(F32), axis=1, keepdims=True)
            sum_ref[i, rows, :] = jnp.broadcast_to(total, (HD, 8))


def attend_back(valid, half, qt, kt, vt, mixed, grad_mixed, stats):
    d, t = qt.shape
    steps = H // HPG // 2
    rows = HPG * HD
    blk = pl.BlockSpec((rows, t), lambda i, v, h: (h[0] * steps + i, 0))
    return pcall(
        attend_back_kernel,
        grid_spec=dict(
            num_scalar_prefetch=2,
            grid=(steps,),
            in_specs=[blk] * 5
            + [pl.BlockSpec((HPG, 8, t), lambda i, v, h: (h[0] * steps + i, 0, 0))],
            out_specs=[
                pl.BlockSpec((3, rows, t), lambda i, v, h: (0, i, 0)),
                pl.BlockSpec((2, rows, 8), lambda i, v, h: (0, i, 0)),
            ],
        ),
        out_shape=[
            jax.ShapeDtypeStruct((3, d // 2, t), BF),
            jax.ShapeDtypeStruct((2, d // 2, 8), F32),
        ],
            cost_estimate=cost(19),
        name="attend_back",
    )(valid, half, qt, kt, vt, mixed, grad_mixed, stats)


def out_project(w, mixed_t, frames, vrows, tile=640):
    d, t = mixed_t.shape
    k = len(w.arrays)
    nt = d // tile

    def kernel(offs, m_ref, x_ref, v_ref, *rest):
        refs = rest[:k]
        mid_ref, low_ref, lowt_ref, buf, sem = rest[k:]
        j = pl.program_id(0)
        slot = stream(w, refs, offs, buf, sem, tile, j)
        out = dg(m_ref[...], buf[slot], 0, 0)
        for s in range(nt):

            @pl.when(j == s)
            def _():
                cols = slice(s * tile, (s + 1) * tile)
                mid_ref[:, cols] = out + x_ref[:, cols].astype(F32) + v_ref[2:3, cols]

        @pl.when(j == nt - 1)
        def _():
            for i in range(t // 128):
                rows = slice(i * 128, (i + 1) * 128)
                v = mid_ref[rows, :]
                c = v - jnp.mean(v, axis=1, keepdims=True)
                r = lax.rsqrt(jnp.mean(c * c, axis=1, keepdims=True) + EPS)
                y = c * r * v_ref[6:7, :] + v_ref[7:8, :]
                low_ref[rows, :] = y.astype(BF)
                lowt_ref[:, rows] = jnp.transpose(y).astype(BF)

    return pcall(
        kernel,
        grid_spec=dict(
            num_scalar_prefetch=1,
            grid=(nt,),
            in_specs=[full((d, t)), full((t, d)), full((8, d))] + [ANY] * k,
            out_specs=[full((t, d)), full((t, d)), full((d, t))],
            scratch_shapes=[pltpu.VMEM((2, d, tile), BF), pltpu.SemaphoreType.DMA((2, k))],
        ),
        out_shape=[
            jax.ShapeDtypeStruct((t, d), F32),
            jax.ShapeDtypeStruct((t, d), BF),
            jax.ShapeDtypeStruct((d, t), BF),
        ],
            cost_estimate=cost(15),
        name="out_project",
    )(w.offs, mixed_t, frames, vrows, *w.arrays)


def gelu_pair(v):
    d = jnp.abs(v) * (0.3275911 * 0.7071067811865476) + 1.0
    k = pl.reciprocal(d, approx=True)
    k = k * (2.0 - d * k)
    e = jnp.exp2(v * v * (-0.5 * LOG2E))
    poly = k * (
        0.5 * 0.254829592
        + k
        * (
            0.5 * -0.284496736
            + k * (0.5 * 1.421413741 + k * (0.5 * -1.453152027 + k * (0.5 * 1.061405429)))
        )
    )
    tail = poly * e
    cdf = jnp.where(v >= 0, 1.0 - tail, tail)
    return v * cdf, cdf + v * e * 0.3989422804014327


def up_project(w, low, bias, tile=1280, sub=256):
    t, d = low.shape
    n = w.cols
    k = len(w.arrays)

    def kernel(offs, x_ref, b_ref, *rest):
        refs = rest[:k]
        h_ref, g_ref, buf, sem = rest[k:]
        slot = stream(w, refs, offs, buf, sem, tile, pl.program_id(0))
        for s in range(tile // sub):
            cols = slice(s * sub, (s + 1) * sub)
            for r, size in chunks_of(t):
                rows = slice(r, r + size)
                before = dg(x_ref[rows, :], buf[slot, :, cols], 1, 0) + b_ref[:, cols]
                hidden, slope = gelu_pair(before)
                h_ref[rows, cols] = hidden.astype(BF)
                g_ref[rows, cols] = slope.astype(BF)

    blk = pl.BlockSpec((t, tile), lambda j, o: (0, j))
    return pcall(
        kernel,
        grid_spec=dict(
            num_scalar_prefetch=1,
            grid=(n // tile,),
            in_specs=[full((t, d)), pl.BlockSpec((1, tile), lambda j, o: (0, j))] + [ANY] * k,
            out_specs=[blk, blk],
            scratch_shapes=[pltpu.VMEM((2, d, tile), BF), pltpu.SemaphoreType.DMA((2, k))],
        ),
        out_shape=[jax.ShapeDtypeStruct((t, n), BF)] * 2,
            cost_estimate=cost(32),
        name="up_project",
    )(w.offs, low, bias, *w.arrays)


def down_back(f, w, cot, slope, tile=1280):
    t, d = cot.shape
    n = slope.shape[1]
    k = len(w.arrays)
    nt = n // tile

    def kernel(offs, f_ref, c_ref, s_ref, *rest):
        refs = rest[:k]
        o_ref, b_ref, buf, sem = rest[k:]
        j = pl.program_id(0)
        copies = w.copies(refs, offs, buf, sem, 0, d)

        @pl.when(j == 0)
        def _():
            start_all(copies)
            wait(copies[:1])

        @pl.when(j == 1)
        def _():
            wait(copies[1:])

        rows = pl.ds(pl.multiple_of(j * tile, tile), tile)
        grad = dg(c_ref[...], buf[rows, :], 1, 1) * s_ref[...].astype(F32)
        low = grad.astype(BF)
        o_ref[...] = low
        b_ref[...] = jnp.sum(low.astype(F32), axis=0, keepdims=True)

    def place(j, o, f):
        return (0, jnp.bitwise_xor(j, f[0]))

    return pcall(
        kernel,
        grid_spec=dict(
            num_scalar_prefetch=2,
            grid=(nt,),
            in_specs=[full((t, d)), pl.BlockSpec((t, tile), place)] + [ANY] * k,
            out_specs=[pl.BlockSpec((t, tile), place), pl.BlockSpec((1, tile), place)],
            scratch_shapes=[pltpu.VMEM((n, d), BF), pltpu.SemaphoreType.DMA((k,))],
        ),
        out_shape=[jax.ShapeDtypeStruct((t, n), BF), jax.ShapeDtypeStruct((1, n), F32)],
            cost_estimate=cost(20),
        name="down_back",
    )(w.offs, f, cot, slope, *w.arrays)


def down_project(f, w, hidden, middle, vrows):
    t, d = middle.shape
    n = hidden.shape[1]
    k = len(w.arrays)
    nb = 4
    blk = n // nb

    def kernel(offs, f_ref, h_ref, m_ref, v_ref, *rest):
        refs = rest[:k]
        o_ref, wbuf, hbuf, mbuf, obuf, wsem, hsem, msem, osem = rest[k:]
        wc = w.copies(refs, offs, wbuf, wsem, 0, d)
        groups = groups_of(t)
        hc = []
        for g, (r, size) in enumerate(groups):
            hc.append([])
            for i in range(nb):
                owner = jnp.bitwise_xor(f_ref[0], i)
                cols = pl.ds(pl.multiple_of(owner * blk, blk), blk)
                here = pl.ds(r, size)
                hc[g].append(
                    pltpu.make_async_copy(
                        h_ref.at[here, cols],
                        hbuf.at[here, pl.ds(i * blk, blk)],
                        hsem.at[g, i],
                    )
                )
        mc = pltpu.make_async_copy(m_ref, mbuf, msem.at[0])
        start_all(hc[0] + wc + [mc] + hc[1] + hc[2])
        oc = []
        for i, (r, size) in enumerate(groups):
            rows = slice(r, r + size)
            wait(hc[i])
            if i == 0:
                wait(wc[:1])
                acc = dg(hbuf[rows, :blk], wbuf[:blk, :], 1, 0)
                wait(wc[1:])
                acc = acc + dg(hbuf[rows, blk:], wbuf[blk:, :], 1, 0)
                wait([mc])
            else:
                acc = dg(hbuf[rows, :], wbuf[...], 1, 0)
            obuf[rows, :] = (acc + mbuf[rows, :] + v_ref[3:4, :]).astype(BF)
            c = pltpu.make_async_copy(obuf.at[rows, :], o_ref.at[rows, :], osem.at[i])
            c.start()
            oc.append(c)
        wait(oc)

    return pcall(
        kernel,
        grid_spec=dict(
            num_scalar_prefetch=2,
            grid=(1,),
            in_specs=[ANY, ANY, full((8, d))] + [ANY] * k,
            out_specs=ANY,
            scratch_shapes=[
                pltpu.VMEM((n, d), BF),
                pltpu.VMEM((t, n), BF),
                pltpu.VMEM((t, d), F32),
                pltpu.VMEM((t, d), BF),
                pltpu.SemaphoreType.DMA((k,)),
                pltpu.SemaphoreType.DMA((3, nb)),
                pltpu.SemaphoreType.DMA((1,)),
                pltpu.SemaphoreType.DMA((8,)),
            ],
        ),
        out_shape=jax.ShapeDtypeStruct((t, d), BF),
            cost_estimate=cost(23),
        name="down_project",
    )(w.offs, f, hidden, middle, vrows, *w.arrays)


def norm_back(v, e, gain):
    c = v - jnp.mean(v, axis=1, keepdims=True)
    r = lax.rsqrt(jnp.mean(c * c, axis=1, keepdims=True) + EPS)
    xhat = c * r
    eg = e * gain
    grad = r * (
        eg
        - jnp.mean(eg, axis=1, keepdims=True)
        - xhat * jnp.mean(eg * xhat, axis=1, keepdims=True)
    )
    return grad, e * xhat


def up_back(w, grad_before, middle, cot, vrows, parts=4):
    t, d = cot.shape
    n = w.cols
    k = len(w.arrays)
    kk = len(w.rows)
    blk = n // parts

    def kernel(offs, gb_ref, m_ref, c_ref, v_ref, *rest):
        refs = rest[:k]
        gm_ref, low_ref, sums_ref = rest[k : k + 3]
        wbuf, gbuf, mbuf, cbuf, obuf, lbuf, wsem, gsem, osem = rest[k + 3 :]
        groups = groups_of(t)
        wc = [
            w.copies(refs, offs, wbuf, wsem.at[i], i * blk, (i + 1) * blk, i * blk)
            for i in range(parts)
        ]

        def rows_of(src, dst, sem):
            return [
                pltpu.make_async_copy(src.at[pl.ds(r, size)], dst.at[pl.ds(r, size)], sem.at[i])
                for i, (r, size) in enumerate(groups)
            ]

        gc, mc, cc = (
            rows_of(*v)
            for v in (
                (gb_ref, gbuf, gsem.at[0]),
                (m_ref, mbuf, gsem.at[1]),
                (c_ref, cbuf, gsem.at[2]),
            )
        )
        start_all(gc[:1])
        for c in wc:
            start_all(c)
        start_all([mc[0], cc[0], gc[1], mc[1], cc[1], gc[2], mc[2], cc[2]])
        oc = []
        sums = [jnp.zeros((1, d), F32)] * 3
        for i, (r, size) in enumerate(groups):
            wait([gc[i]])
            if i == 0:
                e = None
                for p in range(parts):
                    wait(wc[p])
                    cols = slice(p * blk, (p + 1) * blk)
                    part = dg(gbuf[r : r + size, cols], wbuf[:, cols], 1, 1)
                    e = part if e is None else e + part
            else:
                e = dg(gbuf[r : r + size, :], wbuf[...], 1, 1)
            wait([mc[i], cc[i]])
            for q, n128 in chunks_of(size):
                rows = slice(r + q, r + q + n128)
                eq = e[q : q + n128]
                grad, ex = norm_back(mbuf[rows, :], eq, v_ref[6:7, :])
                gm = cbuf[rows, :].astype(F32) + grad
                low = gm.astype(BF)
                obuf[rows, :] = gm
                lbuf[rows, :] = low
                terms = (ex, eq, low.astype(F32))
                sums = [a + jnp.sum(b, axis=0, keepdims=True) for a, b in zip(sums, terms)]
                out = [
                    pltpu.make_async_copy(
                        obuf.at[rows, :], gm_ref.at[rows, :], osem.at[0, len(oc)]
                    ),
                    pltpu.make_async_copy(
                        lbuf.at[rows, :], low_ref.at[rows, :], osem.at[1, len(oc)]
                    ),
                ]
                start_all(out)
                oc.append(out)
        sums_ref[...] = jnp.concatenate(sums + [jnp.zeros((5, d), F32)], axis=0)
        for c in oc:
            wait(c)

    return pcall(
        kernel,
        grid_spec=dict(
            num_scalar_prefetch=1,
            grid=(1,),
            in_specs=[ANY, ANY, ANY, full((8, d))] + [ANY] * k,
            out_specs=[ANY, ANY, full((8, d))],
            scratch_shapes=[
                pltpu.VMEM((d, n), BF),
                pltpu.VMEM((t, n), BF),
                pltpu.VMEM((t, d), F32),
                pltpu.VMEM((t, d), BF),
                pltpu.VMEM((t, d), F32),
                pltpu.VMEM((t, d), BF),
                pltpu.SemaphoreType.DMA((parts, kk)),
                pltpu.SemaphoreType.DMA((3, 3)),
                pltpu.SemaphoreType.DMA((2, 8)),
            ],
        ),
        out_shape=[
            jax.ShapeDtypeStruct((t, d), F32),
            jax.ShapeDtypeStruct((t, d), BF),
            jax.ShapeDtypeStruct((8, d), F32),
        ],
            cost_estimate=cost(28),
        name="up_back",
    )(w.offs, grad_before, middle, cot, vrows, *w.arrays)


def out_back(w, grad_attn):
    t, d = grad_attn.shape
    k = len(w.arrays)

    def kernel(offs, ga_ref, *rest):
        refs = rest[:k]
        o_ref, buf, sem = rest[k:]
        copies = w.copies(refs, offs, buf, sem, 0, w.cols)
        start_all(copies)
        wait(copies)
        o_ref[...] = dg(buf[...], ga_ref[...], 1, 1).astype(BF)

    return pcall(
        kernel,
        grid_spec=dict(
            num_scalar_prefetch=1,
            grid=(1,),
            in_specs=[full((t, d))] + [ANY] * k,
            out_specs=full((d, t)),
            scratch_shapes=[pltpu.VMEM((d, w.cols), BF), pltpu.SemaphoreType.DMA((k,))],
        ),
        out_shape=jax.ShapeDtypeStruct((d, t), BF),
            cost_estimate=cost(9),
        name="out_back",
    )(w.offs, grad_attn, *w.arrays)


def input_back(first, ws, halves, grad_middle, frames, vrows):
    d = 2 * halves[0].shape[1]
    t = halves[0].shape[2]
    k = len(ws[0].arrays)

    def kernel(offs, first_ref, a_ref, b_ref, gm_ref, x_ref, v_ref, *rest):
        refs = [rest[i * k : (i + 1) * k] for i in range(3)]
        o_ref, sums_ref = rest[3 * k : 3 * k + 2]
        wbuf, dbuf, gbuf, xbuf, obuf, wsem, dsem, msem, osem = rest[3 * k + 2 :]
        groups = groups_of(t)
        wc = [ws[i].copies(refs[i], offs, wbuf, wsem.at[i], 0, d, i * d) for i in range(3)]
        dc = []
        for g, (r, size) in enumerate(groups):
            dc.append([])
            for i in range(3):
                for h, ref in enumerate((a_ref, b_ref)):
                    spot = i * d + jnp.bitwise_xor(first_ref[0], h) * (d // 2)
                    dc[g].append(
                        pltpu.make_async_copy(
                            ref.at[i, :, pl.ds(r, size)],
                            dbuf.at[pl.ds(pl.multiple_of(spot, 128), d // 2), pl.ds(r, size)],
                            dsem.at[g, i, h],
                        )
                    )
        mc = [
            pltpu.make_async_copy(gm_ref, gbuf, msem.at[0]),
            pltpu.make_async_copy(x_ref, xbuf, msem.at[1]),
        ]
        start_all(dc[0])
        for c in wc:
            start_all(c)
        start_all(mc + dc[1] + dc[2])
        oc = []
        sums = [jnp.zeros((1, d), F32)] * 2
        for i, (r, size) in enumerate(groups):
            group = slice(r, r + size)
            wait(dc[i])
            if i == 0:
                e = None
                for p in range(3):
                    wait(wc[p])
                    ks = slice(p * d, (p + 1) * d)
                    part = dg(dbuf[ks, group], wbuf[:, ks], 0, 1)
                    e = part if e is None else e + part
                wait(mc)
            else:
                e = dg(dbuf[:, group], wbuf[...], 0, 1)
            for q, n128 in chunks_of(size):
                rows = slice(r + q, r + q + n128)
                eq = e[q : q + n128]
                grad, ex = norm_back(xbuf[rows, :].astype(F32), eq, v_ref[4:5, :])
                obuf[rows, :] = gbuf[rows, :] + grad
                sums = [a + jnp.sum(b, axis=0, keepdims=True) for a, b in zip(sums, (ex, eq))]
                c = pltpu.make_async_copy(obuf.at[rows, :], o_ref.at[rows, :], osem.at[len(oc)])
                c.start()
                oc.append(c)
        sums_ref[...] = jnp.concatenate(sums + [jnp.zeros((6, d), F32)], axis=0)
        wait(oc)

    return pcall(
        kernel,
        grid_spec=dict(
            num_scalar_prefetch=2,
            grid=(1,),
            in_specs=[ANY] * 4 + [full((8, d))] + [ANY] * (3 * k),
            out_specs=[ANY, full((8, d))],
            scratch_shapes=[
                pltpu.VMEM((d, 3 * d), BF),
                pltpu.VMEM((3 * d, t), BF),
                pltpu.VMEM((t, d), F32),
                pltpu.VMEM((t, d), BF),
                pltpu.VMEM((t, d), F32),
                pltpu.SemaphoreType.DMA((3, k)),
                pltpu.SemaphoreType.DMA((3, 3, 2)),
                pltpu.SemaphoreType.DMA((2,)),
                pltpu.SemaphoreType.DMA((8,)),
            ],
        ),
        out_shape=[jax.ShapeDtypeStruct((t, d), F32), jax.ShapeDtypeStruct((8, d), F32)],
            cost_estimate=cost(22),
        name="input_back",
    )(
        ws[0].offs,
        first,
        *halves,
        grad_middle,
        frames,
        vrows,
        *ws[0].arrays,
        *ws[1].arrays,
        *ws[2].arrays,
    )


def wgrad(name, order, side, left, right, mode, addends, groups, owners, sides=2):
    nb = order.shape[0]
    per = nb // groups
    down, heads = mode == "down", mode == "heads"
    if down:
        t, n = left.shape
        blk = n // owners // sides
        width = right.shape[1]
        grid, tile = nb, width
    else:
        d, t = left.shape
        blk = d // owners
        width = right.shape[0] * right.shape[1] if heads else right.shape[1] // 2
        tile = width if heads else min(width, 1280)
        grid = width // tile

    def kernel(order_ref, side_ref, *rest):
        if down:
            i = pl.program_id(0)
            part = dg(rest[0][...], rest[1][...], 0, 0)
            add, outs = rest[2 : 2 + len(addends)], rest[2 + len(addends) :]
            for g in range(groups):

                @pl.when((i >= g * per) & (i < (g + 1) * per))
                def _(g=g):
                    v = part
                    if add:
                        v = v + add[g][...].astype(F32)
                    outs[g][...] = v.astype(BF)

            return
        r_ref = rest[nb]
        add, outs = rest[nb + 1 : nb + 1 + len(addends)], rest[nb + 1 + len(addends) :]
        for g in range(groups):
            lhs = jnp.concatenate([r[...] for r in rest[g * per : (g + 1) * per]], axis=0)
            if heads:
                rhs = r_ref[...].reshape(tile, t)
                v = dg(lhs, rhs, 1, 1)
            else:
                v = dg(lhs, r_ref[...], 1, 0)
            if add:
                v = v + add[g][...].astype(F32)
            outs[g][...] = v.astype(BF)

    rows = per * blk
    if down:

        def out_spec(g):
            return pl.BlockSpec(
                (blk, width), lambda i, o, s: (jnp.clip(i - g * per, 0, per - 1), 0)
            )

        outs = [out_spec(g) for g in range(groups)]
        in_specs = [
            pl.BlockSpec((t, blk), lambda i, o, s: (0, sides * o[i] + s[0])),
            full((t, width)),
        ]
        args = [left, right]
    else:
        outs = [pl.BlockSpec((rows, tile), lambda j, o, s: (0, j))] * groups
        in_specs = [
            pl.BlockSpec((blk, t), functools.partial(lambda b, j, o, s: (o[b], 0), b))
            for b in range(nb)
        ]
        args = [left] * nb + [right]
        if heads:
            in_specs.append(full(right.shape))
        else:
            in_specs.append(pl.BlockSpec((t, tile), lambda j, o, s: (0, s[0] * grid + j)))
    k = right.shape[0] if down else t
    return pcall(
        kernel,
        grid_spec=dict(
            num_scalar_prefetch=2,
            grid=(grid,),
            in_specs=in_specs + outs[: len(addends)],
            out_specs=outs,
        ),
        out_shape=[jax.ShapeDtypeStruct((rows, width), BF)] * groups,
            cost_estimate=cost(COST[name]),
        name=name,
    )(order, side, *args, *addends)


def pick(v, start, rows, deps=None):
    width = v.shape[1]
    parts = 2 if rows % 32 == 0 else 1
    step = rows // parts

    def kernel(start_ref, v_ref, o_ref, buf, sem):
        ins, outs = [], []
        for i in range(parts):
            here = pl.ds(i * step, step)
            row = pl.ds(pl.multiple_of(start_ref[0] + i * step, 16), step)
            ins.append(pltpu.make_async_copy(v_ref.at[row], buf.at[here], sem.at[0, i]))
            outs.append(pltpu.make_async_copy(buf.at[here], o_ref.at[here], sem.at[1, i]))
        start_all(ins)
        for i in range(parts):
            ins[i].wait()
            outs[i].start()
        wait(outs)

    return pcall(
        kernel,
        grid_spec=dict(
            num_scalar_prefetch=1,
            grid=(1,),
            in_specs=[ANY],
            out_specs=ANY,
            scratch_shapes=[pltpu.VMEM((rows, width), v.dtype), pltpu.SemaphoreType.DMA((2, parts))],
        ),
        out_shape=jax.ShapeDtypeStruct((rows, width), v.dtype),
        deps=deps,
        cost_estimate=cost(1.8),
        name="pick",
    )(scalar(start), v)


def land(*values):
    out = pcall(
        lambda *refs: None,
        grid_spec=dict(grid=(1,), in_specs=[ANY] * len(values), out_specs=[ANY] * len(values)),
        out_shape=[jax.ShapeDtypeStruct(v.shape, v.dtype) for v in values],
        aliases={i: i for i in range(len(values))},
        cost_estimate=cost(0.3),
        name="land",
    )(*values)
    return out


def scalar(v):
    return jnp.asarray(v, jnp.int32).reshape(1)


class Relay:
    def __init__(self, net, shard):
        self.net, self.shard = net, shard
        self.rows = shard.shape[0] // 2

    def one(self, later=True):
        v = pick(self.shard, 0, 2 * self.rows) if later else self.shard
        self.s1 = self.net.move(v, "first")

    def one_done(self):
        net = self.net
        (self.s1,) = land(self.s1)
        self.t1 = net.move(self.s1, "core")
        self.s2 = net.move(pick(self.s1, net.c * self.rows, self.rows), "second")

    def two_done(self):
        (self.s2,) = land(self.s2)
        self.t2 = self.net.move(self.s2, "core")

    def weight(self, relative=False):
        net, r = self.net, self.rows
        ways = [0, 1 + net.c, 2 - net.c, 3, 3]
        parts = [0, 0, 0, net.c, 1 - net.c]
        owners = ways if relative else [net.f ^ w for w in ways]
        offs = offsets([o * (2 * r) + q * r for o, q in zip(owners, parts)])
        pieces = [self.shard, self.s1, self.t1, self.s2, self.t2]
        return Weight([(pieces, [0] * 5)], self.shard.shape[1], [2 * r] * 3 + [r] * 2, offs)


def offsets(values):
    return jnp.stack([jnp.asarray(v, jnp.int32) for v in values])


class Reduce:
    def __init__(self, net, make):
        self.net, self.make = net, make

    def theirs(self):
        net = self.net
        parts = self.make(net.order(1 - net.c), net.side(1 - net.c), [], 2)
        self.got = [net.move(p, "core") for p in parts]

    def mine(self):
        net = self.net
        send, self.kept = self.make(net.order(net.c), net.side(net.c), self.got, 2)
        self.p1 = net.move(send, "first")

    def second(self):
        rows = self.kept.shape[0] // 2
        on = combine([(self.kept, None, 1), (self.p1, None, 1)], rows)
        self.p2 = self.net.move(on, "second")


class Replicas:
    def __init__(self, net, r):
        self.net = net
        self.q = r.p2.shape[0] // 4
        self.terms = [r.kept, r.p1, r.p2]

    def own(self, block):
        return [(v, block, 0) for v in self.terms]

    def one(self):
        net = self.net
        v = combine(self.own(1 - net.zlow), 2 * self.q)
        self.r1 = net.move(v, "zlow")

    def two(self):
        net, q = self.net, self.q
        zl, zh = net.zlow, net.zhigh
        v = combine(self.own(2 * zl + 1 - zh) + [(self.r1, 1 - zh, 0)], q)
        self.r2 = net.move(v, "zhigh")

    def three(self):
        net, q = self.net, self.q
        zl, zh = net.zlow, net.zhigh
        self.mine = combine(self.own(2 * zl + zh) + [(self.r1, zh, 0), (self.r2, None, 0)], q)
        self.r3 = net.move(self.mine, "zhigh")
        self.r4 = net.move(self.mine, "zlow")

    def four(self):
        net = self.net
        (self.r3,) = land(self.r3)
        self.r5 = net.move(self.r3, "zlow")
        self.t = [net.move(v, "core") for v in (self.mine, self.r3)]

    def five(self):
        net = self.net
        self.r4, self.r5 = land(self.r4, self.r5)
        self.t += [net.move(v, "core") for v in (self.r4, self.r5)]

    def finish(self, widths, by_rows):
        net = self.net
        zl, zh = net.zlow, net.zhigh
        spots = [2 * zl + zh, 2 * zl + 1 - zh, 2 * (1 - zl) + zh, 2 * (1 - zl) + 1 - zh]
        pieces = [self.mine, self.r3, self.r4, self.r5] + self.t
        return assemble(pieces, offsets(spots + [net.c]), widths, by_rows)


def assemble(pieces, spots, widths, by_rows):
    q, w = pieces[0].shape
    starts = [sum(widths[:i]) for i in range(len(widths))]
    n = len(widths)

    def kernel(spot_ref, *rest):
        ins, outs = rest[:8], rest[8 : 8 + n]
        buf, wide, isem, osem = rest[8 + n :]
        loads = [pltpu.make_async_copy(ins[i], buf.at[i], isem.at[i]) for i in range(8)]
        start_all(loads)
        stores = []
        for i in range(8):
            side = spot_ref[4] if i < 4 else 1 - spot_ref[4]
            loads[i].wait()
            if i >= 2:
                wait(stores[i - 2])
            wide[i % 2] = buf[i].astype(F32)
            out = []
            for j in range(n):
                row = spot_ref[i % 4] * q
                if by_rows:
                    row = row + side * (4 * q)
                    cols = pl.ds(0, widths[j])
                else:
                    cols = pl.ds(pl.multiple_of(side * widths[j], 128), widths[j])
                out.append(
                    pltpu.make_async_copy(
                        wide.at[i % 2, :, pl.ds(starts[j], widths[j])],
                        outs[j].at[pl.ds(pl.multiple_of(row, 8), q), cols],
                        osem.at[i % 2, j],
                    )
                )
            start_all(out)
            stores.append(out)
        wait(stores[6] + stores[7])

    shapes = [(8 * q, v) if by_rows else (4 * q, 2 * v) for v in widths]
    return pcall(
        kernel,
        grid_spec=dict(
            num_scalar_prefetch=1,
            grid=(1,),
            in_specs=[ANY] * 8,
            out_specs=[ANY] * n,
            scratch_shapes=[
                pltpu.VMEM((8, q, w), BF),
                pltpu.VMEM((2, q, w), F32),
                pltpu.SemaphoreType.DMA((8,)),
                pltpu.SemaphoreType.DMA((2, n)),
            ],
        ),
        out_shape=[jax.ShapeDtypeStruct(v, F32) for v in shapes],
        cost_estimate=cost(5),
        name="assemble",
    )(spots, *pieces)


def combine(terms, rows):
    width = terms[0][0].shape[1]
    blk = rows
    while blk * width * 2 > 450 * 1024 and blk % 32 == 0:
        blk //= 2
    per = rows // blk
    moves = [scalar(0 if s is None else s) for _, s, _ in terms]

    def kernel(*refs):
        ins, o_ref = refs[len(terms) : -1], refs[-1]
        total = ins[0][...].astype(F32)
        for r in ins[1:]:
            total = total + r[...].astype(F32)
        o_ref[...] = total.astype(BF)

    def spec(i):
        fixed = terms[i][2] * per
        return pl.BlockSpec((blk, width), lambda j, *s: (s[i][0] * per + fixed + j, 0))

    return pcall(
        kernel,
        grid_spec=dict(
            num_scalar_prefetch=len(terms),
            grid=(per,),
            in_specs=[spec(i) for i in range(len(terms))],
            out_specs=pl.BlockSpec((blk, width), lambda j, *s: (j, 0)),
        ),
        out_shape=jax.ShapeDtypeStruct((rows, width), BF),
        cost_estimate=cost(3),
        name="combine",
    )(*moves, *[t[0] for t in terms])


class Net:
    def __init__(self, n, m):
        self.n, self.m = n, m
        self.f = lax.axis_index("fsdp")
        r = lax.axis_index("rep")
        self.c = r % 2
        self.zlow = (r // 2) % 2
        self.zhigh = r // 4

    def move(self, v, kind):
        pairs = []
        for f in range(self.n):
            for r in range(self.m):
                c = r % 2
                to_f, to_r = f, r
                if kind == "first":
                    to_f = f ^ (1 + c)
                elif kind == "second":
                    to_f = f ^ (2 - c)
                elif kind == "core":
                    to_r = r ^ 1
                elif kind == "zlow":
                    to_r = r ^ 2
                elif kind == "zhigh":
                    to_r = r ^ 4
                else:
                    to_f = f ^ kind
                pairs.append((f * self.m + r, to_f * self.m + to_r))
        out = lax.ppermute(v, AXES, pairs)
        return CLOCK[0].after_next(out) if kind == "core" else out

    def order(self, c):
        a, b = 1 + c, 2 - c
        return jnp.stack([self.f ^ a, self.f ^ 3, self.f, self.f ^ b]).astype(jnp.int32)

    def side(self, c):
        return jnp.asarray(c, jnp.int32)[None]


def merge(values, p):
    width = values[0].shape[1]

    def kernel(*refs):
        total = refs[0][...]
        lane = lax.broadcasted_iota(jnp.int32, (1, width), 1)
        for r in refs[1:-1]:
            v = r[...]
            total = jnp.where(lane < width - p, total + v, jnp.maximum(total, v))
        refs[-1][...] = total

    return pcall(
        kernel,
        grid_spec=dict(
            grid=(1,), in_specs=[full((1, width))] * len(values), out_specs=full((1, width))
        ),
        out_shape=jax.ShapeDtypeStruct((1, width), F32),
        cost_estimate=cost(1),
        name="merge",
    )(*values)


VECTOR_SPOTS = (0, 1, 2, 8, 3, 4, 5, 6, 7)


def finish(own, k, w_query, w_key, threshold, head_peak):
    gv = [own[i * k : (i + 1) * k] for i in range(8)] + [own[8 * k :]]
    limit = threshold[0].astype(F32) / UNIT
    factor = jnp.sqrt(limit / jnp.maximum(head_peak, limit))
    columns = jnp.broadcast_to(factor[:, None], (H, HD)).reshape(1, -1)
    clipped_query = (w_query.astype(F32) * columns).astype(BF)
    clipped_key = (w_key.astype(F32) * columns).astype(BF)
    return tuple(gv[i] for i in VECTOR_SPOTS) + (head_peak, factor, clipped_query, clipped_key)


def per_device(inputs, cotangent, lengths, threshold, *weights):
    n, m = lax.axis_size("fsdp"), lax.axis_size("rep")
    _, t, d = inputs.shape
    frames = inputs.reshape(t, d)
    cot = cotangent.reshape(t, d)
    index = lax.axis_index("fsdp") * m + lax.axis_index("rep")
    valid = lax.dynamic_slice_in_dim(lengths.reshape(-1), index, 1, 0)
    run = on_grid if (n, m) == (4, 8) else on_any
    layer_out, grad_inputs, matrices, vectors = run(
        n, m, frames, cot, valid, threshold, *weights
    )
    return (
        (layer_out.reshape(1, t, d), grad_inputs.reshape(1, t, d)) + tuple(matrices) + vectors
    )


def packed(vecs):
    return jnp.concatenate([vecs[VECTOR_SPOTS.index(i)] for i in range(9)])[None]


def on_grid(n, m, frames, cot, valid, threshold, wq_, wk_, wv_, wo_, wu_, wd_, *vecs):
    CLOCK[0] = clock = Clock(True)
    net = Net(n, m)
    t, d = frames.shape
    ff = wu_.shape[1]
    k = d // n
    h = d // 2
    f = scalar(net.f)
    gq, gk, gv, go, gu, gd = (Relay(net, w) for w in (wq_, wk_, wv_, wo_, wu_, wd_))

    gq.one(False)
    gk.one(False)
    shard = packed(vecs)
    v1, v2 = net.move(shard, "first"), net.move(shard, 3)
    gq.one_done()
    gv.one()
    v1, v2 = land(v1, v2)
    v3 = net.move(v1, "core")
    gk.one_done()
    vrows, vcols, bu = unpack_vectors(
        [shard, jnp.where(net.c == 0, v1, v3), jnp.where(net.c == 0, v3, v1), v2],
        k, ff // n, f,
    )
    normed_t = norm_transposed(frames, vrows)
    gq.two_done()
    clock.wait(gq.t2)
    qt = project(gq.weight(), normed_t, vcols, 0)
    gv.one_done()
    go.one()
    gk.two_done()
    clock.wait(gk.t2)
    kt = project(gk.weight(), normed_t, vcols, None)
    gv.two_done()
    clock.wait(gv.t2)
    vt = project(gv.weight(), normed_t, vcols, 1)
    go.one_done()
    gu.one()
    mixed, stats = attend(valid, qt, kt, vt)
    go.two_done()
    clock.wait(go.t2)
    middle, low, low_t = out_project(go.weight(), mixed, frames, vrows)
    gu.one_done()
    gd.one()
    gu.two_done()
    clock.wait(gu.t2)
    wu = gu.weight()
    hidden, slope = up_project(wu, low, bu)

    def maker(name, left, right, mode):
        def make(order, side, addends, groups):
            return wgrad(name, order, side, left, right, mode, addends, groups, n)

        return make

    rd = Reduce(net, maker("wgrad_down", hidden, cot, "down"))
    rd.theirs()
    gd.one_done()
    rd.mine()
    gd.two_done()
    clock.wait(gd.t2)
    wd = gd.weight(relative=True)
    grad_before, grad_bu = down_back(f, wd, cot, slope)
    ru = Reduce(net, maker("wgrad_up", low_t, grad_before, "cols"))
    ru.theirs()
    grad_middle, grad_attn, sums_ffn = up_back(wu, grad_before, middle, cot, vrows)
    rd.second()
    ru.mine()
    ro = Reduce(net, maker("wgrad_out", mixed, grad_attn, "cols"))
    ro.theirs()
    grad_mixed = out_back(go.weight(), grad_attn)
    ro.mine()
    zd = Replicas(net, rd)
    zd.one()
    theirs, own = net.side(1 - net.c), net.side(net.c)
    g_theirs, sums_theirs = attend_back(valid, theirs, qt, kt, vt, mixed, grad_mixed, stats)
    zd.two()
    halves = [g_theirs, None]

    def make_qkv(order, side, addends, groups):
        right = halves[1] if addends else halves[0]
        return wgrad("wgrad_qkv", order, side, normed_t, right, "heads", addends, groups, n)

    rq = Reduce(net, make_qkv)
    rq.theirs()
    ru.second()
    zd.three()
    halves[1], sums_own = attend_back(valid, own, qt, kt, vt, mixed, grad_mixed, stats)
    rq.mine()
    ro.second()
    zd.four()
    zu = Replicas(net, ru)
    zu.one()
    ws = [g.weight() for g in (gq, gk, gv)]
    grad_inputs, sums_attn = input_back(theirs, ws, halves, grad_middle, frames, vrows)
    rq.second()
    zu.two()
    zo = Replicas(net, ro)
    zo.one()
    zd.five()
    grad_bd = jnp.sum(cot.astype(F32), axis=0, keepdims=True)
    small = pack_vectors(
        f, n, theirs, (sums_theirs, sums_own), sums_ffn, sums_attn, grad_bd, grad_bu, stats
    )
    small = [small[0]] + [net.move(small[i], i) for i in (1, 2, 3)]
    layer_out = down_project(f, wd, hidden, middle, vrows)
    zq = Replicas(net, rq)
    zq.one()
    zu.three()
    zo.two()
    small = merge(small, 128)
    small = [small, net.move(small, "core")]
    (grad_w_down,) = zd.finish([d], True)
    zq.two()
    zo.three()
    zu.four()
    small = merge(small, 128)
    small = [small, net.move(small, "zlow")]
    zq.three()
    zo.four()
    zu.five()
    small = merge(small, 128)
    small = [small, net.move(small, "zhigh")]
    zo.five()
    (grad_w_up,) = zu.finish([ff // 2], False)
    zq.four()
    (grad_w_out,) = zo.finish([h], False)
    small = merge(small, 128)
    zq.five()
    qkv = zq.finish([h] * 3, False)
    vectors = finish(small[0, :-128], k, wq_, wk_, threshold, small[0, -128 : H - 128])
    return layer_out, grad_inputs, (*qkv, grad_w_out, grad_w_up, grad_w_down), vectors


def on_any(n, m, frames, cot, valid, threshold, wq_, wk_, wv_, wo_, wu_, wd_, *vecs):
    CLOCK[0] = Clock(False)
    t, d = frames.shape
    ff = wu_.shape[1]
    zero = jnp.zeros((1,), jnp.int32)
    order = jnp.arange(n, dtype=jnp.int32)

    def gather(shard):
        whole = lax.all_gather(shard, "fsdp", axis=0, tiled=True)
        return Weight([([whole], [0])], whole.shape[1], [whole.shape[0]], zero)

    def reduce(name, left, rights, mode):
        sides = []
        for i, right in enumerate(rights):
            (g,) = wgrad(name, order, zero + i, left, right, mode, [], 1, n, len(rights))
            g = lax.psum_scatter(g, "fsdp", scatter_dimension=0, tiled=True)
            sides.append(lax.psum(g, "rep"))
        return sides

    shard = packed(vecs)
    whole = lax.all_gather(shard, "fsdp", axis=0, tiled=True)
    shards = [whole[i : i + 1] for i in range(n)]
    vrows, vcols, bu = unpack_vectors(shards, d // n, ff // n)
    wq, wk, wv, wo, wu, wd = (gather(w) for w in (wq_, wk_, wv_, wo_, wu_, wd_))
    normed_t = norm_transposed(frames, vrows)
    qt = project(wq, normed_t, vcols, 0)
    kt = project(wk, normed_t, vcols, None)
    vt = project(wv, normed_t, vcols, 1)
    mixed, stats = attend(valid, qt, kt, vt)
    middle, low, low_t = out_project(wo, mixed, frames, vrows)
    hidden, slope = up_project(wu, low, bu)
    grad_before, grad_bu = down_back(zero, wd, cot, slope)
    grad_middle, grad_attn, sums_ffn = up_back(wu, grad_before, middle, cot, vrows)
    grad_mixed = out_back(wo, grad_attn)
    halves, sums = zip(
        *[
            attend_back(valid, zero + i, qt, kt, vt, mixed, grad_mixed, stats)
            for i in range(2)
        ]
    )
    grad_inputs, sums_attn = input_back(
        zero, (wq, wk, wv), halves, grad_middle, frames, vrows
    )
    layer_out = down_project(zero, wd, hidden, middle, vrows)
    down = reduce("wgrad_down", hidden, [cot], "down")
    up = reduce("wgrad_up", low_t, [grad_before] * 2, "cols")
    out = reduce("wgrad_out", mixed, [grad_attn] * 2, "cols")
    qkv = reduce("wgrad_qkv", normed_t, halves, "heads")
    h = d // 2
    matrices = [
        jnp.concatenate([s[:, i * h : (i + 1) * h] for s in qkv], axis=1).astype(F32)
        for i in range(3)
    ] + [
        jnp.concatenate(out, axis=1).astype(F32),
        jnp.concatenate(up, axis=1).astype(F32),
        down[0].astype(F32),
    ]
    grad_bd = jnp.sum(cot.astype(F32), axis=0, keepdims=True)
    rows = pack_vectors(
        zero, n, zero, sums, sums_ffn, sums_attn, grad_bd, grad_bu, stats
    )
    rows = jnp.concatenate(rows, axis=0)
    own = lax.psum_scatter(rows[:, :-128], "fsdp", scatter_dimension=0, tiled=True)
    own = lax.psum(own, "rep")[0]
    peaks = lax.pmax(rows[0, -128:], AXES)[:H]
    vectors = finish(own, d // n, wq_, wk_, threshold, peaks)
    return layer_out, grad_inputs, matrices, vectors


def solution(mesh):
    tokens = P(None, AXES, None)
    mat = P("fsdp", None)
    vec = P("fsdp")
    return jax.shard_map(
        per_device,
        mesh=mesh,
        in_specs=(tokens, tokens, P(), P()) + (mat,) * 6 + (vec,) * 9,
        out_specs=(tokens, tokens) + (mat,) * 6 + (vec,) * 9 + (P(), P(), mat, mat),
        check_vma=False,
    )
```
